32 devices in a mesh: sub: 8 (over z, x), tile: 4 (over y, core).
Axes of the slice: x: 2, y: 2, z: 4, core: 2. Of those that a mesh axis runs over, the one named last changes fastest.
Arguments:
- echoes: bfloat16 [2, 4096, 4096], P(None, 'sub', 'tile'), may hold values from -6 to 6
- image: float32 [2, 256, 128, 128], P(None, ('sub', 'tile')), may hold values from -6 to 6
- merge_own: bfloat16 [3, 2, 4096, 128], P(None, None, 'sub'), may hold values from -0.25 to 0.25
- merge_pair: bfloat16 [3, 2, 4096, 128], P(None, None, 'sub'), may hold values from -0.25 to 0.25
- merge_angle: float32 [3, 4096], P(None, 'sub'), may hold values from -3.140625 to 3.140625
- beam_kernel: bfloat16 [128, 128], replicated, may hold values from -0.5 to 0.5
- range_kernel: bfloat16 [128, 128], replicated, may hold values from -0.5 to 0.5
- block_map: int32 [32, 32, 2], P('sub', 'tile'), may hold values from 0 to 31, as said below
- route_angle: float32 [32, 32, 2], P('sub', 'tile'), may hold values from -3.140625 to 3.140625
Outputs:
- new_image: float32 [2, 256, 128, 128], P(None, ('sub', 'tile'))
- residual: bfloat16 [2, 4096, 4096], P(None, 'sub', 'tile')
The draws below stay inside these ranges and needn't reach their ends.
Inputs may be any that keep to these rules, and one draw needn't show every extreme that they name: `block_map`: each entry names one of the 32 image tiles of the polar tile's own beam sector, counted from the sector's first tile; every tile of every sector is named at least once.
All inputs are finite; a program needn't handle non-finite values.
Results may differ from the reference program's by a relative error of at most 0.017.
Values may be sent and summed in bfloat16 or wider, within the bound.
A program may use at most 64 MiB of HBM per device.

```python
import jax
import jax.numpy as jnp
from jax import lax

BLOCK = 128
BEAM_DEV = 512
SECTIONS = 3
HITS = 2
BEAMS = 4096
RANGE = 4096
REGION = 32
TILES = 256
N_SUB = 8


def draw_block_map(key, part):
    key = jax.random.fold_in(key, 7)
    key_left, key_right, key_shift = jax.random.split(key, 3)
    row_blocks = BEAMS // BLOCK
    col_blocks = RANGE // BLOCK
    left_draw = jax.random.randint(key_left, (row_blocks, col_blocks, HITS), 0, REGION)
    right_draw = jax.random.randint(key_right, (row_blocks, col_blocks, HITS), 0, REGION)
    skewed = left_draw * right_draw // REGION
    sectors = BEAMS // BEAM_DEV
    per_sector = skewed.reshape(sectors, -1)
    offsets = jax.random.randint(key_shift, (sectors, 1), 0, REGION)
    covered = (jnp.arange(REGION)[None, :] + offsets) % REGION
    per_sector = per_sector.at[:, :REGION].set(covered)
    return per_sector.reshape(row_blocks, col_blocks, HITS).astype(jnp.int32)


def level_of(key, shape, cuts, smallest, high):
    def one(position, shards_of):
        heights = jax.random.uniform(jax.random.fold_in(jax.random.fold_in(key, 6), position), (shards_of,), jnp.float32, smallest / len(cuts), high / len(cuts))
        return jnp.repeat(jnp.exp(heights), shape[position] // shards_of).reshape((-1,) + (1,) * (len(shape) - position - 1))

    level = one(*cuts[0])
    for cut in cuts[1:]:
        level = level * one(*cut)
    return level


def noise(own_key, dims, scale, bound, cuts=(), dtype=jnp.bfloat16):
    values = scale * jax.random.normal(own_key, dims, jnp.float32)
    if cuts:
        values = values * level_of(own_key, dims, cuts, -0.22, 0.18)
    return jnp.clip(values, -bound, bound).astype(dtype)


def setup_inputs(seed: int = 0) -> dict:
    splits = jax.random.split(jax.random.key(seed), 10)
    return {
        "echoes": noise(splits[0], (2, BEAMS, RANGE), 1.0, 6.0, ((1, 8), (2, 4))),
        "image": noise(splits[1], (2, TILES, BLOCK, BLOCK), 1.0, 6.0, ((1, 32),), jnp.float32),
        "merge_own": noise(splits[2], (SECTIONS, 2, BEAMS, BLOCK), (4 * BLOCK) ** -0.5, 0.25, ((2, 8),)),
        "merge_pair": noise(splits[3], (SECTIONS, 2, BEAMS, BLOCK), (4 * BLOCK) ** -0.5, 0.25, ((2, 8),)),
        "merge_angle": jnp.clip(jax.random.uniform(splits[4], (SECTIONS, BEAMS), jnp.float32, -3.140625, 3.140625), -3.140625, 3.140625),
        "beam_kernel": noise(splits[5], (BLOCK, BLOCK), BLOCK ** -0.5, 0.5),
        "range_kernel": noise(splits[6], (BLOCK, BLOCK), BLOCK ** -0.5, 0.5),
        "block_map": draw_block_map(jax.random.fold_in(splits[9], 71), 0),
        "route_angle": jnp.clip(jax.random.uniform(splits[8], (BEAMS // BLOCK, RANGE // BLOCK, HITS), jnp.float32, -3.140625, 3.140625), -3.140625, 3.140625),
    }


highest = lax.Precision.HIGHEST
step_length = 0.1


def blockwise(matrix, field, adjoint):
    blocks = matrix.astype(jnp.float32).reshape(2, -1, BLOCK, BLOCK)
    values = field.astype(jnp.float32).reshape(2, blocks.shape[1], BLOCK, field.shape[2])
    pattern = "nac,nar->ncr" if adjoint else "nac,ncr->nar"

    def multiply(left_op, right_op):
        return jnp.einsum(pattern, left_op, right_op, precision=highest)

    real_real = multiply(blocks[0], values[0])
    imag_imag = multiply(blocks[1], values[1])
    real_imag = multiply(blocks[0], values[1])
    imag_real = multiply(blocks[1], values[0])
    if adjoint:
        real_out, imag_out = real_real + imag_imag, real_imag - imag_real
    else:
        real_out, imag_out = real_real - imag_imag, real_imag + imag_real
    rows_all = field.shape[1]
    return jnp.stack([real_out.reshape(rows_all, -1), imag_out.reshape(rows_all, -1)])


def swapped(field, section):
    partner = jnp.bitwise_xor(jnp.arange(N_SUB), 1 << section)
    shaped = field.reshape(2, N_SUB, BEAM_DEV, field.shape[2])
    return shaped[:, partner].reshape(field.shape)


def to_tiles(field):
    shaped = field.reshape(2, field.shape[1] // BLOCK, BLOCK, field.shape[2] // BLOCK, BLOCK)
    return shaped.transpose(0, 1, 3, 2, 4)


def from_tiles(tiles):
    shaped = tiles.transpose(0, 1, 3, 2, 4)
    return shaped.reshape(2, tiles.shape[1] * BLOCK, tiles.shape[2] * BLOCK)


def reference(echoes, image, merge_own, merge_pair, merge_angle, beam_kernel, range_kernel, block_map, route_angle):
    rho = (jnp.arange(RANGE).astype(jnp.float32) + 0.5) / RANGE
    phase_list = []
    for section in range(SECTIONS):
        theta = merge_angle[section][:, None] * rho[None, :]
        phase_list.append((jnp.cos(theta), jnp.sin(theta)))
    image_half = image.astype(jnp.bfloat16)
    sector = jnp.arange(BEAMS // BLOCK) // (BEAM_DEV // BLOCK)
    targets = sector[:, None, None] * REGION + block_map

    def route_row(inputs):
        index_row, angle_row = inputs
        picked = image_half[:, index_row].astype(jnp.float32)
        cos_row = jnp.cos(angle_row)[:, :, None, None]
        sin_row = jnp.sin(angle_row)[:, :, None, None]
        real_sum = jnp.sum(cos_row * picked[0] + sin_row * picked[1], axis=1)
        imag_sum = jnp.sum(cos_row * picked[1] - sin_row * picked[0], axis=1)
        return jnp.stack([real_sum, imag_sum]).astype(jnp.bfloat16)

    routed = lax.map(route_row, (targets, route_angle)).transpose(1, 0, 2, 3, 4)
    beam_f = beam_kernel.astype(jnp.float32)
    range_f = range_kernel.astype(jnp.float32)
    half_forward = jnp.einsum("pijac,dc->pijad", routed.astype(jnp.float32), range_f, precision=highest).astype(jnp.bfloat16)
    polar = jnp.einsum("ka,pijkd->pijad", beam_f, half_forward.astype(jnp.float32), precision=highest).astype(jnp.bfloat16)
    level = from_tiles(polar)
    for section in reversed(range(SECTIONS)):
        phase_cos, phase_sin = phase_list[section]
        level_f = level.astype(jnp.float32)
        turned = jnp.stack([phase_cos * level_f[0] + phase_sin * level_f[1],
                            phase_cos * level_f[1] - phase_sin * level_f[0]]).astype(jnp.bfloat16)
        own_part = blockwise(merge_own[section], turned, True)
        pair_part = blockwise(merge_pair[section], turned, True).astype(jnp.bfloat16)
        level = (own_part + swapped(pair_part, section).astype(jnp.float32)).astype(jnp.bfloat16)
    residual = (level.astype(jnp.float32) - echoes.astype(jnp.float32)).astype(jnp.bfloat16)
    field = residual
    for section in range(SECTIONS):
        phase_cos, phase_sin = phase_list[section]
        mixed = blockwise(merge_own[section], field, False) + blockwise(merge_pair[section], swapped(field, section), False)
        field = jnp.stack([phase_cos * mixed[0] - phase_sin * mixed[1],
                           phase_cos * mixed[1] + phase_sin * mixed[0]]).astype(jnp.bfloat16)
    tiles = to_tiles(field)
    beamed = jnp.einsum("ak,pijkc->pijac", beam_f, tiles.astype(jnp.float32), precision=highest).astype(jnp.bfloat16)
    spread = jnp.einsum("pijac,cd->pijad", beamed.astype(jnp.float32), range_f, precision=highest).astype(jnp.bfloat16)
    spread_f = spread.astype(jnp.float32)
    gradient = jnp.zeros((2, TILES, BLOCK, BLOCK), jnp.float32)
    for hit in range(HITS):
        cos_hit = jnp.cos(route_angle[:, :, hit])[:, :, None, None]
        sin_hit = jnp.sin(route_angle[:, :, hit])[:, :, None, None]
        real_part = cos_hit * spread_f[0] - sin_hit * spread_f[1]
        imag_part = cos_hit * spread_f[1] + sin_hit * spread_f[0]
        flat_targets = targets[:, :, hit].reshape(-1)
        gradient = gradient.at[:, flat_targets].add(jnp.stack([real_part, imag_part]).reshape(2, -1, BLOCK, BLOCK))
    new_image = image - step_length * gradient
    return (new_image, residual)
```

```python
import functools

import jax
import jax.numpy as jnp
from jax import lax
from jax.experimental import pallas as pl
from jax.experimental.pallas import tpu as pltpu
from jax.sharding import PartitionSpec as P

step_length = 0.1
f32 = jnp.float32
bf16 = jnp.bfloat16
MESH = pl.DeviceIdType.MESH

LAGS = (0, 2, 3, 4, 5, 6, 8, 9)


def kernel(
    sizes,
    map_ref,
    cos_ref,
    sin_ref,
    echoes_ref,
    image_ref,
    own_ref,
    pair_ref,
    angle_ref,
    turn_ref,
    beam_ref,
    beam_t_ref,
    range_ref,
    range_t_ref,
    weight_ref,
    new_ref,
    residual_ref,
    region,
    back_mat,
    fore_mat,
    phases,
    held,
    sendbuf,
    recvbuf,
    spread,
    total,
    weights,
    mat_sem,
    g_send,
    g_recv,
    w_send,
    w_recv,
    x_send,
    x_recv,
    s_send,
    s_recv,
):
    tiles, chunks, rows_n, side, sections, owned, hits = sizes
    stages = 2 * sections
    me_t = lax.axis_index("tile")
    me_s = lax.axis_index("sub")

    def partner(bit):
        width = 1 << bit
        return me_s + width - 2 * width * ((me_s // width) % 2)

    bits = [sections - 1 - n if n < sections else n - sections for n in range(stages)]

    def mat_copy(which, k, i):
        ref = own_ref if which == 0 else pair_ref
        return pltpu.make_async_copy(
            ref.at[k, :, i], spread.at[me_t, which * sections + k, i], mat_sem.at[which, k, i]
        )

    for which in range(2):
        for k in range(sections):
            for i in range(rows_n):
                mat_copy(which, k, i).start()

    barrier = pltpu.get_barrier_semaphore()
    for d in range(1, tiles):
        pl.semaphore_signal(
            barrier, inc=1, device_id={"tile": (me_t + d) % tiles}, device_id_type=MESH
        )
    for bit in range(sections):
        pl.semaphore_signal(barrier, inc=1, device_id={"sub": partner(bit)}, device_id_type=MESH)

    def convert(u, carry):
        for p in range(2):
            region[me_t * owned + u, p] = image_ref[p, u].astype(bf16)
        return carry

    lax.fori_loop(0, owned, convert, 0)
    pl.semaphore_wait(barrier, tiles - 1 + sections)

    def region_copy(d, src):
        return pltpu.make_async_remote_copy(
            src_ref=region.at[pl.ds(src * owned, owned)],
            dst_ref=region.at[pl.ds(src * owned, owned)],
            send_sem=g_send.at[d],
            recv_sem=g_recv.at[src],
            device_id={"tile": (me_t + d) % tiles},
            device_id_type=MESH,
        )

    def weight_copy(d, src):
        dest = (me_t + d) % tiles
        return pltpu.make_async_remote_copy(
            src_ref=weight_ref.at[dest],
            dst_ref=weights.at[src],
            send_sem=w_send.at[d],
            recv_sem=w_recv.at[src],
            device_id={"tile": dest},
            device_id_type=MESH,
        )

    for d in range(1, tiles):
        region_copy(d, me_t).start()
    for d in range(1, tiles):
        weight_copy(d, me_t).start()
    weights[me_t] = weight_ref[me_t]

    base = lax.convert_element_type(me_t * (chunks * side), f32)
    total_range = tiles * chunks * side
    for k in range(sections):

        def start_phase(i, carry, k=k):
            col = lax.broadcasted_iota(jnp.int32, (side, side), 1).astype(f32)
            rho = (base + col + 0.5) / total_range
            theta = angle_ref[k, i] * rho
            c, s = jnp.cos(theta), jnp.sin(theta)
            phases[sections - 1 - k, 0, i] = c
            phases[sections - 1 - k, 1, i] = s
            phases[sections + k, 0, i] = c
            phases[sections + k, 1, i] = s
            return carry

        lax.fori_loop(0, rows_n, start_phase, 0)

    for k in range(sections):
        for i in range(rows_n):
            for which in range(2):
                mat_copy(which, k, i).wait()

    for k in range(sections):

        def build(i, carry, k=k):
            for which in range(2):
                slot = which * sections + k
                real = spread[me_t, slot, i, 0]
                imag = spread[me_t, slot, i, 1]
                real_t = real.astype(f32).T.astype(bf16)
                imag_t = imag.astype(f32).T.astype(bf16)
                lo = 2 * side * which
                back_mat[k, i, pl.ds(lo, side), pl.ds(0, side)] = real_t
                back_mat[k, i, pl.ds(lo, side), pl.ds(side, side)] = imag_t
                back_mat[k, i, pl.ds(lo + side, side), pl.ds(0, side)] = -imag_t
                back_mat[k, i, pl.ds(lo + side, side), pl.ds(side, side)] = real_t
                fore_mat[k, i, pl.ds(0, side), pl.ds(lo, side)] = real
                fore_mat[k, i, pl.ds(0, side), pl.ds(lo + side, side)] = -imag
                fore_mat[k, i, pl.ds(side, side), pl.ds(lo, side)] = imag
                fore_mat[k, i, pl.ds(side, side), pl.ds(lo + side, side)] = real
            return carry

        lax.fori_loop(0, rows_n, build, 0)

    def zero(u, carry):
        total[u] = jnp.zeros_like(total[u])
        return carry

    lax.fori_loop(0, owned, zero, 0)

    for d in range(1, tiles):
        region_copy(d, (me_t + d) % tiles).wait_recv()
    for d in range(1, tiles):
        weight_copy(d, (me_t + d) % tiles).wait_recv()

    def exchange(n, c):
        return pltpu.make_async_remote_copy(
            src_ref=sendbuf.at[c],
            dst_ref=recvbuf.at[n, c],
            send_sem=x_send.at[n, c],
            recv_sem=x_recv.at[n, c],
            device_id={"sub": partner(bits[n])},
            device_id_type=MESH,
        )

    def dot(a, b):
        return jnp.dot(a, b, preferred_element_type=f32)

    def advance(n, i, k):
        c, s = phases[n, 0, i], phases[n, 1, i]
        dc, ds = turn_ref[0, k, i], turn_ref[1, k, i]
        phases[n, 0, i] = c * dc - s * ds
        phases[n, 1, i] = s * dc + c * ds
        return c, s

    def merge_back(n, c, i, level_real, level_imag):
        k = bits[n]
        pc, ps = advance(n, i, k)
        lr, li = level_real.astype(f32), level_imag.astype(f32)
        turned = jnp.concatenate([pc * lr + ps * li, pc * li - ps * lr], axis=0).astype(bf16)
        out = dot(back_mat[k, i], turned)
        held[c, i] = out[: 2 * side].reshape(2, side, side)
        sendbuf[c, i] = out[2 * side :].astype(bf16).reshape(2, side, side)

    def stage_first(c):
        def body(i, carry):
            real = jnp.zeros((side, side), f32)
            imag = jnp.zeros((side, side), f32)
            for h in range(hits):
                at = (i * chunks + c) * hits + h
                q = map_ref[at]
                cc, ss = cos_ref[at], sin_ref[at]
                pr = region[q, 0].astype(f32)
                pi = region[q, 1].astype(f32)
                real += cc * pr + ss * pi
                imag += cc * pi - ss * pr
            routed = jnp.concatenate([real, imag], axis=0).astype(bf16)
            half = dot(routed, range_t_ref[...]).astype(bf16)
            polar_r = dot(beam_t_ref[...], half[:side]).astype(bf16)
            polar_i = dot(beam_t_ref[...], half[side:]).astype(bf16)
            merge_back(0, c, i, polar_r, polar_i)
            return carry

        lax.fori_loop(0, rows_n, body, 0)
        exchange(0, c).start()

    def stage_back(n, c):
        exchange(n - 1, c).wait()

        def body(i, carry):
            level = (held[c, i] + recvbuf[n - 1, c, i].astype(f32)).astype(bf16)
            merge_back(n, c, i, level[0], level[1])
            return carry

        lax.fori_loop(0, rows_n, body, 0)
        exchange(n, c).start()

    def stage_residual(c):
        n = sections
        exchange(n - 1, c).wait()
        cols = pl.ds(pl.multiple_of(c * side, side), side)

        def body(i, carry):
            rows = pl.ds(pl.multiple_of(i * side, side), side)
            level = (held[c, i] + recvbuf[n - 1, c, i].astype(f32)).astype(bf16)
            res = (level.astype(f32) - echoes_ref[:, rows, cols].astype(f32)).astype(bf16)
            residual_ref[:, rows, cols] = res
            sendbuf[c, i] = res
            return carry

        lax.fori_loop(0, rows_n, body, 0)
        exchange(n, c).start()

    def merge_fore(n, c, i):
        k = bits[n]
        values = jnp.concatenate(
            [
                sendbuf[c, i].reshape(2 * side, side),
                recvbuf[n, c, i].reshape(2 * side, side),
            ],
            axis=0,
        )
        mixed = dot(fore_mat[k, i], values)
        mr, mi = mixed[:side], mixed[side:]
        pc, ps = advance(n, i, k)
        return jnp.concatenate([pc * mr - ps * mi, pc * mi + ps * mr], axis=0).astype(bf16)

    def stage_fore(n, c):
        exchange(n, c).wait()

        def body(i, carry):
            sendbuf[c, i] = merge_fore(n, c, i).reshape(2, side, side)
            return carry

        lax.fori_loop(0, rows_n, body, 0)
        exchange(n + 1, c).start()

    def spread_copy(d, src, c):
        return pltpu.make_async_remote_copy(
            src_ref=spread.at[src, c],
            dst_ref=spread.at[src, c],
            send_sem=s_send.at[d, c],
            recv_sem=s_recv.at[src, c],
            device_id={"tile": (me_t + d) % tiles},
            device_id_type=MESH,
        )

    def stage_last(c):
        n = stages - 1
        exchange(n, c).wait()

        def body(i, carry):
            field = merge_fore(n, c, i)
            beamed = jnp.concatenate(
                [dot(beam_ref[...], field[:side]), dot(beam_ref[...], field[side:])], axis=0
            ).astype(bf16)
            out = dot(beamed, range_ref[...]).astype(bf16)
            spread[me_t, c, i] = out.reshape(2, side, side)
            return carry

        lax.fori_loop(0, rows_n, body, 0)
        for d in range(1, tiles):
            spread_copy(d, me_t, c).start()

    part = 16

    def stage_gather(c):
        for d in range(1, tiles):
            spread_copy(d, (me_t + d) % tiles, c).wait_recv()

        def body(b, carry):
            rows = pl.ds(pl.multiple_of(b * part, part), part)
            reals = [total[u, 0, rows] for u in range(owned)]
            imags = [total[u, 1, rows] for u in range(owned)]

            def add(t, sums):
                reals, imags = list(sums[0]), list(sums[1])
                for i in range(rows_n):
                    sr = spread[t, c, i, 0, rows].astype(f32)
                    si = spread[t, c, i, 1, rows].astype(f32)
                    for u in range(owned):
                        wc = weights[t, 0, c * rows_n + i, pl.ds(u, 1)]
                        ws = weights[t, 1, c * rows_n + i, pl.ds(u, 1)]
                        reals[u] += wc * sr - ws * si
                        imags[u] += wc * si + ws * sr
                return tuple(reals), tuple(imags)

            reals, imags = lax.fori_loop(0, tiles, add, (tuple(reals), tuple(imags)))
            for u in range(owned):
                total[u, 0, rows] = reals[u]
                total[u, 1, rows] = imags[u]
            return carry

        lax.fori_loop(0, side // part, body, 0)

    runs = [stage_first]
    for n in range(1, sections):
        runs.append(functools.partial(stage_back, n))
    runs.append(stage_residual)
    for n in range(sections, stages - 1):
        runs.append(functools.partial(stage_fore, n))
    runs.append(stage_last)
    runs.append(stage_gather)

    def step(t, carry):
        for run, lag in zip(runs, LAGS):
            c = t - lag

            @pl.when((c >= 0) & (c < chunks))
            def _():
                run(c)

        return carry

    lax.fori_loop(0, chunks + LAGS[-1], step, 0)

    def finish(u, carry):
        for p in range(2):
            new_ref[p, u] = image_ref[p, u] - step_length * total[u, p]
        return carry

    lax.fori_loop(0, owned, finish, 0)

    for d in range(1, tiles):
        region_copy(d, me_t).wait_send()
        weight_copy(d, me_t).wait_send()

    def drain(c, carry):
        for d in range(1, tiles):
            spread_copy(d, me_t, c).wait_send()
        return carry

    lax.fori_loop(0, chunks, drain, 0)


def per_device(
    echoes,
    image,
    merge_own,
    merge_pair,
    merge_angle,
    beam_kernel,
    range_kernel,
    block_map,
    route_angle,
):
    side = beam_kernel.shape[0]
    sections = merge_own.shape[0]
    rows_n, chunks, hits = block_map.shape
    tiles = lax.axis_size("tile")
    owned = image.shape[1]
    stages = 2 * sections
    beams = echoes.shape[1]
    total_range = echoes.shape[2] * tiles

    own = merge_own.reshape(sections, 2, rows_n, side, side)
    pair = merge_pair.reshape(sections, 2, rows_n, side, side)
    angle = jnp.broadcast_to(merge_angle[:, :, None], (sections, beams, side)).reshape(
        sections, rows_n, side, side
    )
    delta = merge_angle * (side / total_range)
    turn = jnp.broadcast_to(
        jnp.stack([jnp.cos(delta), jnp.sin(delta)])[..., None], (2, sections, beams, side)
    ).reshape(2, sections, rows_n, side, side)
    route_cos = jnp.cos(route_angle)
    route_sin = jnp.sin(route_angle)
    region_count = tiles * owned
    matched = (block_map[..., None] == jnp.arange(region_count)).astype(f32)
    one = jnp.stack(
        [
            jnp.sum(matched * route_cos[..., None], axis=2),
            jnp.sum(matched * route_sin[..., None], axis=2),
        ]
    )
    one = one.reshape(2, rows_n, chunks, tiles, owned).transpose(3, 0, 2, 1, 4)
    weight = jnp.broadcast_to(
        one.reshape(tiles, 2, chunks * rows_n, owned, 1),
        (tiles, 2, chunks * rows_n, owned, side),
    )
    smem = pl.BlockSpec(memory_space=pltpu.SMEM)
    vmem = pl.BlockSpec(memory_space=pltpu.VMEM)
    hbm = pl.BlockSpec(memory_space=pl.ANY)
    block = (2, side, side)
    dma = pltpu.SemaphoreType.DMA
    return pl.pallas_call(
        functools.partial(kernel, (tiles, chunks, rows_n, side, sections, owned, hits)),
        out_shape=(
            jax.ShapeDtypeStruct(image.shape, f32),
            jax.ShapeDtypeStruct(echoes.shape, bf16),
        ),
        in_specs=[smem] * 3 + [vmem, vmem, hbm, hbm] + [vmem] * 7,
        out_specs=(vmem, vmem),
        scratch_shapes=[
            pltpu.VMEM((region_count,) + block, bf16),
            pltpu.VMEM((sections, rows_n, 4 * side, 2 * side), bf16),
            pltpu.VMEM((sections, rows_n, 2 * side, 4 * side), bf16),
            pltpu.VMEM((stages, 2, rows_n, side, side), f32),
            pltpu.VMEM((chunks, rows_n) + block, f32),
            pltpu.VMEM((chunks, rows_n) + block, bf16),
            pltpu.VMEM((stages, chunks, rows_n) + block, bf16),
            pltpu.VMEM((tiles, chunks, rows_n) + block, bf16),
            pltpu.VMEM((owned,) + block, f32),
            pltpu.VMEM((tiles, 2, chunks * rows_n, owned, side), f32),
            dma((2, sections, rows_n)),
            dma((tiles,)),
            dma((tiles,)),
            dma((tiles,)),
            dma((tiles,)),
            dma((stages, chunks)),
            dma((stages, chunks)),
            dma((tiles, chunks)),
            dma((tiles, chunks)),
        ],
        compiler_params=pltpu.CompilerParams(
            collective_id=0, has_side_effects=True, vmem_limit_bytes=63 * 1024 * 1024
        ),
    )(
        block_map.reshape(-1),
        route_cos.reshape(-1),
        route_sin.reshape(-1),
        echoes,
        image,
        own,
        pair,
        angle,
        turn,
        beam_kernel,
        beam_kernel.T,
        range_kernel,
        range_kernel.T,
        weight,
    )


def solution(mesh):
    return jax.shard_map(
        per_device,
        mesh=mesh,
        in_specs=(
            P(None, "sub", "tile"),
            P(None, ("sub", "tile"), None, None),
            P(None, None, "sub", None),
            P(None, None, "sub", None),
            P(None, "sub"),
            P(),
            P(),
            P("sub", "tile", None),
            P("sub", "tile", None),
        ),
        out_specs=(P(None, ("sub", "tile"), None, None), P(None, "sub", "tile")),
        check_vma=False,
    )
```

```python
import functools

import jax
import jax.numpy as jnp
from jax import lax
from jax.experimental import pallas as pl
from jax.experimental.pallas import tpu as pltpu
from jax.sharding import PartitionSpec as P

step_length = 0.1
f32 = jnp.float32
bf16 = jnp.bfloat16
MESH = pl.DeviceIdType.MESH

LAGS = (0, 1, 2, 3, 4, 5, 6, 7, 8)


def kernel(
    sizes,
    map_ref,
    cos_ref,
    sin_ref,
    echoes_ref,
    image_ref,
    own_ref,
    pair_ref,
    turn_ref,
    beam_ref,
    range_ref,
    weight_ref,
    new_ref,
    residual_ref,
    beam_t_ref,
    range_t_ref,
    region,
    back_mat,
    fore_mat,
    phases,
    held,
    sendbuf,
    recvbuf,
    spread,
    total,
    weights,
    mat_sem,
    g_send,
    g_recv,
    w_send,
    w_recv,
    x_send,
    x_recv,
    s_send,
    s_recv,
):
    tiles, chunks, rows_n, side, sections, owned, hits = sizes
    stages = 2 * sections
    me_t = lax.axis_index("tile")
    me_s = lax.axis_index("sub")

    def partner(bit):
        width = 1 << bit
        return me_s + width - 2 * width * ((me_s // width) % 2)

    bits = [sections - 1 - n if n < sections else n - sections for n in range(stages)]

    def mat_copy(which, k, i):
        ref = own_ref if which == 0 else pair_ref
        return pltpu.make_async_copy(
            ref.at[k, :, pl.ds(i * side, side)], spread.at[me_t, which * sections + k, i], mat_sem.at[which, k, i]
        )

    for which in range(2):
        for k in range(sections):
            for i in range(rows_n):
                mat_copy(which, k, i).start()

    barrier = pltpu.get_barrier_semaphore()
    for d in range(1, tiles):
        pl.semaphore_signal(
            barrier, inc=1, device_id={"tile": (me_t + d) % tiles}, device_id_type=MESH
        )
    for bit in range(sections):
        pl.semaphore_signal(barrier, inc=1, device_id={"sub": partner(bit)}, device_id_type=MESH)

    def convert(u, carry):
        for p in range(2):
            region[me_t * owned + u, p] = image_ref[p, u].astype(bf16)
        return carry

    lax.fori_loop(0, owned, convert, 0)
    pl.semaphore_wait(barrier, tiles - 1 + sections)

    sibling = me_t + 1 - 2 * (me_t % 2)

    def region_copy(d, src, dest):
        return pltpu.make_async_remote_copy(
            src_ref=region.at[pl.ds(src * owned, owned)],
            dst_ref=region.at[pl.ds(src * owned, owned)],
            send_sem=g_send.at[d],
            recv_sem=g_recv.at[src],
            device_id={"tile": dest},
            device_id_type=MESH,
        )

    def weight_copy(d, src):
        dest = (me_t + d) % tiles
        return pltpu.make_async_remote_copy(
            src_ref=weight_ref.at[dest],
            dst_ref=weights.at[src],
            send_sem=w_send.at[d],
            recv_sem=w_recv.at[src],
            device_id={"tile": dest},
            device_id_type=MESH,
        )

    for d in range(2, tiles, 2):
        region_copy(d, me_t, (me_t + d) % tiles).start()
    region_copy(1, me_t, sibling).start()
    weights[me_t] = weight_ref[me_t]
    beam_t_ref[...] = beam_ref[...].astype(f32).T.astype(bf16)
    range_t_ref[...] = range_ref[...].astype(f32).T.astype(bf16)

    base = lax.convert_element_type(me_t * (chunks * side), f32)
    total_range = tiles * chunks * side
    for k in range(sections):

        def start_phase(i, carry, k=k):
            col = lax.broadcasted_iota(jnp.int32, (side, side), 1).astype(f32)
            rho = (base + col + 0.5) / total_range
            theta = turn_ref[2, k, i] * rho
            c, s = jnp.cos(theta), jnp.sin(theta)
            phases[sections - 1 - k, 0, i] = c
            phases[sections - 1 - k, 1, i] = s
            phases[sections + k, 0, i] = c
            phases[sections + k, 1, i] = s
            return carry

        lax.fori_loop(0, rows_n, start_phase, 0)

    for d in range(2, tiles, 2):
        src = (me_t + d) % tiles
        region_copy(d, src, src).wait_recv()
        region_copy(d + 1, src, sibling).start()

    for k in range(sections):
        for i in range(rows_n):
            for which in range(2):
                mat_copy(which, k, i).wait()

    for k in range(sections):

        def build(i, carry, k=k):
            for which in range(2):
                slot = which * sections + k
                real = spread[me_t, slot, i, 0]
                imag = spread[me_t, slot, i, 1]
                real_t = real.astype(f32).T.astype(bf16)
                imag_t = imag.astype(f32).T.astype(bf16)
                lo = 2 * side * which
                back_mat[k, i, pl.ds(lo, side), pl.ds(0, side)] = real_t
                back_mat[k, i, pl.ds(lo, side), pl.ds(side, side)] = imag_t
                back_mat[k, i, pl.ds(lo + side, side), pl.ds(0, side)] = -imag_t
                back_mat[k, i, pl.ds(lo + side, side), pl.ds(side, side)] = real_t
                fore_mat[k, i, pl.ds(0, side), pl.ds(lo, side)] = real
                fore_mat[k, i, pl.ds(0, side), pl.ds(lo + side, side)] = -imag
                fore_mat[k, i, pl.ds(side, side), pl.ds(lo, side)] = imag
                fore_mat[k, i, pl.ds(side, side), pl.ds(lo + side, side)] = real
            return carry

        lax.fori_loop(0, rows_n, build, 0)

    def zero(u, carry):
        total[u] = jnp.zeros_like(total[u])
        return carry

    lax.fori_loop(0, owned, zero, 0)

    for d in range(2, tiles, 2):
        region_copy(d + 1, (sibling + d) % tiles, sibling).wait_recv()
    region_copy(1, sibling, sibling).wait_recv()
    for d in range(1, tiles):
        weight_copy(d, me_t).start()

    def exchange(n, c):
        return pltpu.make_async_remote_copy(
            src_ref=sendbuf.at[c],
            dst_ref=recvbuf.at[n, c],
            send_sem=x_send.at[n, c],
            recv_sem=x_recv.at[n, c],
            device_id={"sub": partner(bits[n])},
            device_id_type=MESH,
        )

    def dot(a, b):
        return jnp.dot(a, b, preferred_element_type=f32)

    def advance(n, i, k):
        c, s = phases[n, 0, i], phases[n, 1, i]
        dc, ds = turn_ref[0, k, i], turn_ref[1, k, i]
        phases[n, 0, i] = c * dc - s * ds
        phases[n, 1, i] = s * dc + c * ds
        return c, s

    def merge_back(n, c, i, level_real, level_imag):
        k = bits[n]
        pc, ps = advance(n, i, k)
        lr, li = level_real.astype(f32), level_imag.astype(f32)
        turned = jnp.concatenate([pc * lr + ps * li, pc * li - ps * lr], axis=0).astype(bf16)
        out = dot(back_mat[k, i], turned)
        held[c, i] = out[: 2 * side].reshape(2, side, side)
        sendbuf[c, i] = out[2 * side :].astype(bf16).reshape(2, side, side)

    def stage_first(c):
        def body(i, carry):
            real = jnp.zeros((side, side), f32)
            imag = jnp.zeros((side, side), f32)
            for h in range(hits):
                q = map_ref[i, c, h]
                cc, ss = cos_ref[i, c, h], sin_ref[i, c, h]
                pr = region[q, 0].astype(f32)
                pi = region[q, 1].astype(f32)
                real += cc * pr + ss * pi
                imag += cc * pi - ss * pr
            routed = jnp.concatenate([real, imag], axis=0).astype(bf16)
            half = dot(routed, range_t_ref[...]).astype(bf16)
            polar_r = dot(beam_t_ref[...], half[:side]).astype(bf16)
            polar_i = dot(beam_t_ref[...], half[side:]).astype(bf16)
            merge_back(0, c, i, polar_r, polar_i)
            return carry

        lax.fori_loop(0, rows_n, body, 0)
        exchange(0, c).start()

    def stage_back(n, c):
        exchange(n - 1, c).wait()

        def body(i, carry):
            level = (held[c, i] + recvbuf[n - 1, c, i].astype(f32)).astype(bf16)
            merge_back(n, c, i, level[0], level[1])
            return carry

        lax.fori_loop(0, rows_n, body, 0)
        exchange(n, c).start()

    def stage_residual(c):
        n = sections
        exchange(n - 1, c).wait()
        cols = pl.ds(pl.multiple_of(c * side, side), side)

        def body(i, carry):
            rows = pl.ds(pl.multiple_of(i * side, side), side)
            level = (held[c, i] + recvbuf[n - 1, c, i].astype(f32)).astype(bf16)
            res = (level.astype(f32) - echoes_ref[:, rows, cols].astype(f32)).astype(bf16)
            residual_ref[:, rows, cols] = res
            sendbuf[c, i] = res
            return carry

        lax.fori_loop(0, rows_n, body, 0)
        exchange(n, c).start()

    def merge_fore(n, c, i):
        k = bits[n]
        values = jnp.concatenate(
            [
                sendbuf[c, i].reshape(2 * side, side),
                recvbuf[n, c, i].reshape(2 * side, side),
            ],
            axis=0,
        )
        mixed = dot(fore_mat[k, i], values)
        mr, mi = mixed[:side], mixed[side:]
        pc, ps = advance(n, i, k)
        return jnp.concatenate([pc * mr - ps * mi, pc * mi + ps * mr], axis=0).astype(bf16)

    def stage_fore(n, c):
        exchange(n, c).wait()

        def body(i, carry):
            sendbuf[c, i] = merge_fore(n, c, i).reshape(2, side, side)
            return carry

        lax.fori_loop(0, rows_n, body, 0)
        exchange(n + 1, c).start()

    def spread_copy(d, src, dest, c):
        return pltpu.make_async_remote_copy(
            src_ref=spread.at[src, c],
            dst_ref=spread.at[src, c],
            send_sem=s_send.at[d, c],
            recv_sem=s_recv.at[src, c],
            device_id={"tile": dest},
            device_id_type=MESH,
        )

    def stage_last(c):
        n = stages - 1
        exchange(n, c).wait()

        def body(i, carry):
            field = merge_fore(n, c, i)
            beamed = jnp.concatenate(
                [dot(beam_ref[...], field[:side]), dot(beam_ref[...], field[side:])], axis=0
            ).astype(bf16)
            out = dot(beamed, range_ref[...]).astype(bf16)
            spread[me_t, c, i] = out.reshape(2, side, side)
            return carry

        lax.fori_loop(0, rows_n, body, 0)
        for d in range(2, tiles, 2):
            spread_copy(d, me_t, (me_t + d) % tiles, c).start()
        spread_copy(1, me_t, sibling, c).start()

    def stage_relay(c):
        for d in range(2, tiles, 2):
            src = (me_t + d) % tiles
            spread_copy(d, src, src, c).wait_recv()
            spread_copy(d + 1, src, sibling, c).start()

    part = 16

    def stage_gather(c):
        for d in range(2, tiles, 2):
            spread_copy(d + 1, (sibling + d) % tiles, sibling, c).wait_recv()
        spread_copy(1, sibling, sibling, c).wait_recv()

        @pl.when(c == 0)
        def _():
            for d in range(1, tiles):
                weight_copy(d, (me_t + d) % tiles).wait_recv()

        def body(b, carry):
            rows = pl.ds(pl.multiple_of(b * part, part), part)
            reals = [total[u, 0, rows] for u in range(owned)]
            imags = [total[u, 1, rows] for u in range(owned)]

            def add(t, sums):
                reals, imags = list(sums[0]), list(sums[1])
                for i in range(rows_n):
                    sr = spread[t, c, i, 0, rows].astype(f32)
                    si = spread[t, c, i, 1, rows].astype(f32)
                    for u in range(owned):
                        wc = weights[t, 0, c * rows_n + i, pl.ds(u, 1)]
                        ws = weights[t, 1, c * rows_n + i, pl.ds(u, 1)]
                        reals[u] += wc * sr - ws * si
                        imags[u] += wc * si + ws * sr
                return tuple(reals), tuple(imags)

            reals, imags = lax.fori_loop(0, tiles, add, (tuple(reals), tuple(imags)))
            for u in range(owned):
                total[u, 0, rows] = reals[u]
                total[u, 1, rows] = imags[u]
            return carry

        lax.fori_loop(0, side // part, body, 0)

    runs = [stage_first]
    for n in range(1, sections):
        runs.append(functools.partial(stage_back, n))
    runs.append(stage_residual)
    for n in range(sections, stages - 1):
        runs.append(functools.partial(stage_fore, n))
    runs.append(stage_last)
    runs.append(stage_relay)
    runs.append(stage_gather)

    def step(t, carry):
        for run, lag in zip(runs, LAGS):
            c = t - lag

            @pl.when((c >= 0) & (c < chunks))
            def _():
                run(c)

        return carry

    lax.fori_loop(0, chunks + LAGS[-1], step, 0)

    def finish(u, carry):
        for p in range(2):
            new_ref[p, u] = image_ref[p, u] - step_length * total[u, p]
        return carry

    lax.fori_loop(0, owned, finish, 0)

    for d in range(1, tiles):
        region_copy(d, me_t, sibling).wait_send()
        weight_copy(d, me_t).wait_send()

    def drain(c, carry):
        for d in range(1, tiles):
            spread_copy(d, me_t, sibling, c).wait_send()
        return carry

    lax.fori_loop(0, chunks, drain, 0)


def per_device(
    echoes,
    image,
    merge_own,
    merge_pair,
    merge_angle,
    beam_kernel,
    range_kernel,
    block_map,
    route_angle,
):
    side = beam_kernel.shape[0]
    sections = merge_own.shape[0]
    rows_n, chunks, hits = block_map.shape
    tiles = lax.axis_size("tile")
    owned = image.shape[1]
    stages = 2 * sections
    beams = echoes.shape[1]
    total_range = echoes.shape[2] * tiles

    delta = merge_angle * (side / total_range)
    turn = jnp.broadcast_to(
        jnp.stack([jnp.cos(delta), jnp.sin(delta), merge_angle])[..., None],
        (3, sections, beams, side),
    ).reshape(3, sections, rows_n, side, side)
    route_cos = jnp.cos(route_angle)
    route_sin = jnp.sin(route_angle)
    region_count = tiles * owned
    matched = (block_map[..., None] == jnp.arange(region_count)).astype(f32)
    one = jnp.stack(
        [
            jnp.sum(matched * route_cos[..., None], axis=2),
            jnp.sum(matched * route_sin[..., None], axis=2),
        ]
    )
    one = one.reshape(2, rows_n, chunks, tiles, owned).transpose(3, 0, 2, 1, 4)
    weight = jnp.broadcast_to(
        one.reshape(tiles, 2, chunks * rows_n, owned, 1),
        (tiles, 2, chunks * rows_n, owned, side),
    )
    smem = pl.BlockSpec(memory_space=pltpu.SMEM)
    vmem = pl.BlockSpec(memory_space=pltpu.VMEM)
    hbm = pl.BlockSpec(memory_space=pl.ANY)
    block = (2, side, side)
    dma = pltpu.SemaphoreType.DMA
    return pl.pallas_call(
        functools.partial(kernel, (tiles, chunks, rows_n, side, sections, owned, hits)),
        out_shape=(
            jax.ShapeDtypeStruct(image.shape, f32),
            jax.ShapeDtypeStruct(echoes.shape, bf16),
        ),
        in_specs=[smem] * 3 + [vmem, vmem, hbm, hbm] + [vmem] * 4,
        out_specs=(vmem, vmem),
        scratch_shapes=[
            pltpu.VMEM((side, side), bf16),
            pltpu.VMEM((side, side), bf16),
            pltpu.VMEM((region_count,) + block, bf16),
            pltpu.VMEM((sections, rows_n, 4 * side, 2 * side), bf16),
            pltpu.VMEM((sections, rows_n, 2 * side, 4 * side), bf16),
            pltpu.VMEM((stages, 2, rows_n, side, side), f32),
            pltpu.VMEM((chunks, rows_n) + block, f32),
            pltpu.VMEM((chunks, rows_n) + block, bf16),
            pltpu.VMEM((stages, chunks, rows_n) + block, bf16),
            pltpu.VMEM((tiles, chunks, rows_n) + block, bf16),
            pltpu.VMEM((owned,) + block, f32),
            pltpu.VMEM((tiles, 2, chunks * rows_n, owned, side), f32),
            dma((2, sections, rows_n)),
            dma((tiles,)),
            dma((tiles,)),
            dma((tiles,)),
            dma((tiles,)),
            dma((stages, chunks)),
            dma((stages, chunks)),
            dma((tiles, chunks)),
            dma((tiles, chunks)),
        ],
        compiler_params=pltpu.CompilerParams(
            collective_id=0, has_side_effects=True, vmem_limit_bytes=63 * 1024 * 1024
        ),
    )(
        block_map,
        route_cos,
        route_sin,
        echoes,
        image,
        merge_own,
        merge_pair,
        turn,
        beam_kernel,
        range_kernel,
        weight,
    )


def solution(mesh):
    return jax.shard_map(
        per_device,
        mesh=mesh,
        in_specs=(
            P(None, "sub", "tile"),
            P(None, ("sub", "tile"), None, None),
            P(None, None, "sub", None),
            P(None, None, "sub", None),
            P(None, "sub"),
            P(),
            P(),
            P("sub", "tile", None),
            P("sub", "tile", None),
        ),
        out_specs=(P(None, ("sub", "tile"), None, None), P(None, "sub", "tile")),
        check_vma=False,
    )
```

```python
import functools

import jax
import jax.numpy as jnp
from jax import lax
from jax.experimental import pallas as pl
from jax.experimental.pallas import tpu as pltpu
from jax.sharding import PartitionSpec as P

step_length = 0.1
PARTS = 2
f32 = jnp.float32
bf16 = jnp.bfloat16
MESH = pl.DeviceIdType.MESH

LAGS = (0, 1, 2, 3, 4, 5, 6, 7, 8)


def kernel(
    sizes,
    map_ref,
    route_ref,
    echoes_ref,
    image_ref,
    own_ref,
    pair_ref,
    angle_ref,
    beam_ref,
    range_ref,
    weight_ref,
    new_ref,
    residual_ref,
    beam_t_ref,
    range_t_ref,
    turn_ref,
    region,
    back_mat,
    fore_mat,
    phases,
    held,
    sendbuf,
    recvbuf,
    spread,
    total,
    weights,
    mat_sem,
    g_send,
    g_recv,
    w_send,
    w_recv,
    x_send,
    x_recv,
    s_send,
    s_recv,
):
    tiles, chunks, rows_n, side, sections, owned, hits = sizes
    stages = 2 * sections
    me_t = lax.axis_index("tile")
    me_s = lax.axis_index("sub")

    def partner(bit):
        width = 1 << bit
        return me_s + width - 2 * width * ((me_s // width) % 2)

    bits = [sections - 1 - n if n < sections else n - sections for n in range(stages)]

    def mat_copy(which, k, i):
        ref = own_ref if which == 0 else pair_ref
        return pltpu.make_async_copy(
            ref.at[k, :, pl.ds(i * side, side)], spread.at[me_t, which * sections + k, i], mat_sem.at[which, k, i]
        )

    for which in range(2):
        for k in range(sections):
            for i in range(rows_n):
                mat_copy(which, k, i).start()

    barrier = pltpu.get_barrier_semaphore()
    for d in range(1, tiles):
        pl.semaphore_signal(
            barrier, inc=1, device_id={"tile": (me_t + d) % tiles}, device_id_type=MESH
        )
    for bit in range(sections):
        pl.semaphore_signal(barrier, inc=1, device_id={"sub": partner(bit)}, device_id_type=MESH)

    def convert(u, carry):
        for p in range(2):
            region[me_t * owned + u, p] = image_ref[p, u].astype(bf16)
        return carry

    lax.fori_loop(0, owned, convert, 0)
    pl.semaphore_wait(barrier, tiles - 1 + sections)

    sibling = me_t + 1 - 2 * (me_t % 2)

    def region_copy(d, src, dest):
        return pltpu.make_async_remote_copy(
            src_ref=region.at[pl.ds(src * owned, owned)],
            dst_ref=region.at[pl.ds(src * owned, owned)],
            send_sem=g_send.at[d],
            recv_sem=g_recv.at[src],
            device_id={"tile": dest},
            device_id_type=MESH,
        )

    def weight_copy(d, src):
        dest = (me_t + d) % tiles
        return pltpu.make_async_remote_copy(
            src_ref=weight_ref.at[dest],
            dst_ref=weights.at[src],
            send_sem=w_send.at[d],
            recv_sem=w_recv.at[src],
            device_id={"tile": dest},
            device_id_type=MESH,
        )

    for d in range(2, tiles, 2):
        region_copy(d, me_t, (me_t + d) % tiles).start()
    region_copy(1, me_t, sibling).start()
    weights[me_t] = weight_ref[me_t]
    beam_t_ref[...] = beam_ref[...].astype(f32).T.astype(bf16)
    range_t_ref[...] = range_ref[...].astype(f32).T.astype(bf16)

    base = lax.convert_element_type(me_t * (chunks * side), f32)
    total_range = tiles * chunks * side

    def prepare(k):
        for i in range(rows_n):
            for which in range(2):
                mat_copy(which, k, i).wait()

        def build(i, carry):
            col = lax.broadcasted_iota(jnp.int32, (side, side), 1).astype(f32)
            rho = (base + col + 0.5) / total_range
            row = angle_ref[pl.ds(k * rows_n + i, 1)]
            delta = row * (side / total_range)
            theta = jnp.broadcast_to(row, (side, side)).T * rho
            turn_ref[0, k, i] = jnp.broadcast_to(jnp.cos(delta), (side, side)).T
            turn_ref[1, k, i] = jnp.broadcast_to(jnp.sin(delta), (side, side)).T
            c, s = jnp.cos(theta), jnp.sin(theta)
            phases[sections - 1 - k, 0, i] = c
            phases[sections - 1 - k, 1, i] = s
            phases[sections + k, 0, i] = c
            phases[sections + k, 1, i] = s
            for which in range(2):
                slot = which * sections + k
                real = spread[me_t, slot, i, 0]
                imag = spread[me_t, slot, i, 1]
                real_t = real.astype(f32).T.astype(bf16)
                imag_t = imag.astype(f32).T.astype(bf16)
                lo = 2 * side * which
                back_mat[k, i, pl.ds(lo, side), pl.ds(0, side)] = real_t
                back_mat[k, i, pl.ds(lo, side), pl.ds(side, side)] = imag_t
                back_mat[k, i, pl.ds(lo + side, side), pl.ds(0, side)] = -imag_t
                back_mat[k, i, pl.ds(lo + side, side), pl.ds(side, side)] = real_t
                fore_mat[k, i, pl.ds(0, side), pl.ds(lo, side)] = real
                fore_mat[k, i, pl.ds(0, side), pl.ds(lo + side, side)] = -imag
                fore_mat[k, i, pl.ds(side, side), pl.ds(lo, side)] = imag
                fore_mat[k, i, pl.ds(side, side), pl.ds(lo + side, side)] = real
            return carry

        lax.fori_loop(0, rows_n, build, 0)

    prepare(sections - 1)
    for d in range(2, tiles, 2):
        src = (me_t + d) % tiles
        region_copy(d, src, src).wait_recv()
        region_copy(d + 1, src, sibling).start()

    def zero(u, carry):
        total[u] = jnp.zeros_like(total[u])
        return carry

    lax.fori_loop(0, owned, zero, 0)

    for d in range(2, tiles, 2):
        region_copy(d + 1, (sibling + d) % tiles, sibling).wait_recv()
    region_copy(1, sibling, sibling).wait_recv()
    for d in range(1, tiles):
        weight_copy(d, me_t).start()

    share = rows_n // PARTS

    def exchange(n, c, part):
        rows = pl.ds(part * share, share)
        return pltpu.make_async_remote_copy(
            src_ref=sendbuf.at[c, rows],
            dst_ref=recvbuf.at[n, c, rows],
            send_sem=x_send.at[n, c, part],
            recv_sem=x_recv.at[n, c, part],
            device_id={"sub": partner(bits[n])},
            device_id_type=MESH,
        )

    def dot(a, b):
        return jnp.dot(a, b, preferred_element_type=f32)

    def advance(n, i, k):
        c, s = phases[n, 0, i], phases[n, 1, i]
        dc, ds = turn_ref[0, k, i], turn_ref[1, k, i]
        phases[n, 0, i] = c * dc - s * ds
        phases[n, 1, i] = s * dc + c * ds
        return c, s

    def merge_back(n, c, i, level_real, level_imag):
        k = bits[n]
        pc, ps = advance(n, i, k)
        lr, li = level_real.astype(f32), level_imag.astype(f32)
        turned = jnp.concatenate([pc * lr + ps * li, pc * li - ps * lr], axis=0).astype(bf16)
        out = dot(back_mat[k, i], turned)
        held[c, i] = out[: 2 * side].reshape(2, side, side)
        sendbuf[c, i] = out[2 * side :].astype(bf16).reshape(2, side, side)

    def stage_first(c):
        def body(i, carry):
            real = jnp.zeros((side, side), f32)
            imag = jnp.zeros((side, side), f32)
            for h in range(hits):
                q = map_ref[i, c, h]
                cc, ss = route_ref[0, i, c, h], route_ref[1, i, c, h]
                pr = region[q, 0].astype(f32)
                pi = region[q, 1].astype(f32)
                real += cc * pr + ss * pi
                imag += cc * pi - ss * pr
            routed = jnp.concatenate([real, imag], axis=0).astype(bf16)
            half = dot(routed, range_t_ref[...]).astype(bf16)
            polar_r = dot(beam_t_ref[...], half[:side]).astype(bf16)
            polar_i = dot(beam_t_ref[...], half[side:]).astype(bf16)
            merge_back(0, c, i, polar_r, polar_i)
            return carry

        for part in range(PARTS):
            lax.fori_loop(part * share, (part + 1) * share, body, 0)
            exchange(0, c, part).start()

    def stage_back(n, c):

        def body(i, carry):
            level = (held[c, i] + recvbuf[n - 1, c, i].astype(f32)).astype(bf16)
            merge_back(n, c, i, level[0], level[1])
            return carry

        for part in range(PARTS):
            exchange(n - 1, c, part).wait()
            lax.fori_loop(part * share, (part + 1) * share, body, 0)
            exchange(n, c, part).start()

    def stage_residual(c):
        n = sections
        cols = pl.ds(pl.multiple_of(c * side, side), side)

        def body(i, carry):
            rows = pl.ds(pl.multiple_of(i * side, side), side)
            level = (held[c, i] + recvbuf[n - 1, c, i].astype(f32)).astype(bf16)
            res = (level.astype(f32) - echoes_ref[:, rows, cols].astype(f32)).astype(bf16)
            residual_ref[:, rows, cols] = res
            sendbuf[c, i] = res
            return carry

        for part in range(PARTS):
            exchange(n - 1, c, part).wait()
            lax.fori_loop(part * share, (part + 1) * share, body, 0)
            exchange(n, c, part).start()

    def merge_fore(n, c, i):
        k = bits[n]
        values = jnp.concatenate(
            [
                sendbuf[c, i].reshape(2 * side, side),
                recvbuf[n, c, i].reshape(2 * side, side),
            ],
            axis=0,
        )
        mixed = dot(fore_mat[k, i], values)
        mr, mi = mixed[:side], mixed[side:]
        pc, ps = advance(n, i, k)
        return jnp.concatenate([pc * mr - ps * mi, pc * mi + ps * mr], axis=0).astype(bf16)

    def stage_fore(n, c):

        def body(i, carry):
            sendbuf[c, i] = merge_fore(n, c, i).reshape(2, side, side)
            return carry

        for part in range(PARTS):
            exchange(n, c, part).wait()
            lax.fori_loop(part * share, (part + 1) * share, body, 0)
            exchange(n + 1, c, part).start()

    def spread_copy(d, src, dest, c):
        return pltpu.make_async_remote_copy(
            src_ref=spread.at[src, c],
            dst_ref=spread.at[src, c],
            send_sem=s_send.at[d, c],
            recv_sem=s_recv.at[src, c],
            device_id={"tile": dest},
            device_id_type=MESH,
        )

    def stage_last(c):
        n = stages - 1

        def body(i, carry):
            field = merge_fore(n, c, i)
            beamed = jnp.concatenate(
                [dot(beam_ref[...], field[:side]), dot(beam_ref[...], field[side:])], axis=0
            ).astype(bf16)
            out = dot(beamed, range_ref[...]).astype(bf16)
            spread[me_t, c, i] = out.reshape(2, side, side)
            return carry

        for part in range(PARTS):
            exchange(n, c, part).wait()
            lax.fori_loop(part * share, (part + 1) * share, body, 0)
        for d in range(2, tiles, 2):
            spread_copy(d, me_t, (me_t + d) % tiles, c).start()
        spread_copy(1, me_t, sibling, c).start()

    def stage_relay(c):
        for d in range(2, tiles, 2):
            src = (me_t + d) % tiles
            spread_copy(d, src, src, c).wait_recv()
            spread_copy(d + 1, src, sibling, c).start()

    height = 16

    def stage_gather(c):
        for d in range(2, tiles, 2):
            spread_copy(d + 1, (sibling + d) % tiles, sibling, c).wait_recv()
        spread_copy(1, sibling, sibling, c).wait_recv()

        @pl.when(c == 0)
        def _():
            for d in range(1, tiles):
                weight_copy(d, (me_t + d) % tiles).wait_recv()

        def body(b, carry):
            rows = pl.ds(pl.multiple_of(b * height, height), height)
            reals = [total[u, 0, rows] for u in range(owned)]
            imags = [total[u, 1, rows] for u in range(owned)]

            def add(t, sums):
                reals, imags = list(sums[0]), list(sums[1])
                for i in range(rows_n):
                    sr = spread[t, c, i, 0, rows].astype(f32)
                    si = spread[t, c, i, 1, rows].astype(f32)
                    for u in range(owned):
                        wc = weights[t, 0, c * rows_n + i, pl.ds(u, 1)]
                        ws = weights[t, 1, c * rows_n + i, pl.ds(u, 1)]
                        reals[u] += wc * sr - ws * si
                        imags[u] += wc * si + ws * sr
                return tuple(reals), tuple(imags)

            reals, imags = lax.fori_loop(0, tiles, add, (tuple(reals), tuple(imags)))
            for u in range(owned):
                total[u, 0, rows] = reals[u]
                total[u, 1, rows] = imags[u]
            return carry

        lax.fori_loop(0, side // height, body, 0)

    runs = [stage_first]
    for n in range(1, sections):
        runs.append(functools.partial(stage_back, n))
    runs.append(stage_residual)
    for n in range(sections, stages - 1):
        runs.append(functools.partial(stage_fore, n))
    runs.append(stage_last)
    runs.append(stage_relay)
    runs.append(stage_gather)

    def step(t, carry):
        for run, lag in zip(runs, LAGS):
            c = t - lag

            @pl.when((c >= 0) & (c < chunks))
            def _():
                run(c)

            if run is stage_first:

                @pl.when(t == 0)
                def _():
                    for k in reversed(range(sections - 1)):
                        prepare(k)

        return carry

    lax.fori_loop(0, chunks + LAGS[-1], step, 0)

    def finish(u, carry):
        for p in range(2):
            new_ref[p, u] = image_ref[p, u] - step_length * total[u, p]
        return carry

    lax.fori_loop(0, owned, finish, 0)

    for d in range(1, tiles):
        region_copy(d, me_t, sibling).wait_send()
        weight_copy(d, me_t).wait_send()

    def drain(c, carry):
        for d in range(1, tiles):
            spread_copy(d, me_t, sibling, c).wait_send()
        return carry

    lax.fori_loop(0, chunks, drain, 0)


def per_device(
    echoes,
    image,
    merge_own,
    merge_pair,
    merge_angle,
    beam_kernel,
    range_kernel,
    block_map,
    route_angle,
):
    side = beam_kernel.shape[0]
    sections = merge_own.shape[0]
    rows_n, chunks, hits = block_map.shape
    tiles = lax.axis_size("tile")
    owned = image.shape[1]
    stages = 2 * sections

    route_cos = jnp.cos(route_angle)
    route_sin = jnp.sin(route_angle)
    region_count = tiles * owned
    matched = (block_map[..., None] == jnp.arange(region_count)).astype(f32)
    one = jnp.stack(
        [
            jnp.sum(matched * route_cos[..., None], axis=2),
            jnp.sum(matched * route_sin[..., None], axis=2),
        ]
    )
    one = one.reshape(2, rows_n, chunks, tiles, owned).transpose(3, 0, 2, 1, 4)
    weight = jnp.broadcast_to(
        one.reshape(tiles, 2, chunks * rows_n, owned, 1),
        (tiles, 2, chunks * rows_n, owned, side),
    )
    smem = pl.BlockSpec(memory_space=pltpu.SMEM)
    vmem = pl.BlockSpec(memory_space=pltpu.VMEM)
    hbm = pl.BlockSpec(memory_space=pl.ANY)
    block = (2, side, side)
    dma = pltpu.SemaphoreType.DMA
    return pl.pallas_call(
        functools.partial(kernel, (tiles, chunks, rows_n, side, sections, owned, hits)),
        out_shape=(
            jax.ShapeDtypeStruct(image.shape, f32),
            jax.ShapeDtypeStruct(echoes.shape, bf16),
        ),
        in_specs=[smem] * 2 + [vmem, vmem, hbm, hbm] + [vmem] * 4,
        out_specs=(vmem, vmem),
        scratch_shapes=[
            pltpu.VMEM((side, side), bf16),
            pltpu.VMEM((side, side), bf16),
            pltpu.VMEM((2, sections, rows_n, side, side), f32),
            pltpu.VMEM((region_count,) + block, bf16),
            pltpu.VMEM((sections, rows_n, 4 * side, 2 * side), bf16),
            pltpu.VMEM((sections, rows_n, 2 * side, 4 * side), bf16),
            pltpu.VMEM((stages, 2, rows_n, side, side), f32),
            pltpu.VMEM((chunks, rows_n) + block, f32),
            pltpu.VMEM((chunks, rows_n) + block, bf16),
            pltpu.VMEM((stages, chunks, rows_n) + block, bf16),
            pltpu.VMEM((tiles, chunks, rows_n) + block, bf16),
            pltpu.VMEM((owned,) + block, f32),
            pltpu.VMEM((tiles, 2, chunks * rows_n, owned, side), f32),
            dma((2, sections, rows_n)),
            dma((tiles,)),
            dma((tiles,)),
            dma((tiles,)),
            dma((tiles,)),
            dma((stages, chunks, PARTS)),
            dma((stages, chunks, PARTS)),
            dma((tiles, chunks)),
            dma((tiles, chunks)),
        ],
        compiler_params=pltpu.CompilerParams(
            collective_id=0, has_side_effects=True, vmem_limit_bytes=63 * 1024 * 1024
        ),
    )(
        block_map,
        jnp.stack([route_cos, route_sin]),
        echoes,
        image,
        merge_own,
        merge_pair,
        merge_angle.reshape(sections * rows_n, side),
        beam_kernel,
        range_kernel,
        weight,
    )


def solution(mesh):
    return jax.shard_map(
        per_device,
        mesh=mesh,
        in_specs=(
            P(None, "sub", "tile"),
            P(None, ("sub", "tile"), None, None),
            P(None, None, "sub", None),
            P(None, None, "sub", None),
            P(None, "sub"),
            P(),
            P(),
            P("sub", "tile", None),
            P("sub", "tile", None),
        ),
        out_specs=(P(None, ("sub", "tile"), None, None), P(None, "sub", "tile")),
        check_vma=False,
    )
```

```python
import functools

import jax
import jax.numpy as jnp
from jax import lax
from jax.experimental import pallas as pl
from jax.experimental.pallas import tpu as pltpu
from jax.sharding import PartitionSpec as P

step_length = 0.1
PARTS = 2
f32 = jnp.float32
bf16 = jnp.bfloat16
MESH = pl.DeviceIdType.MESH

LAGS = (0, 1, 2, 3, 4, 5, 6, 7, 8)


def kernel(
    sizes,
    map_ref,
    route_ref,
    echoes_ref,
    image_ref,
    own_ref,
    pair_ref,
    angle_ref,
    beam_ref,
    range_ref,
    weight_ref,
    new_ref,
    residual_ref,
    beam_t_ref,
    range_t_ref,
    turn_ref,
    region,
    back_mat,
    fore_mat,
    phases,
    held,
    sendbuf,
    recvbuf,
    spread,
    total,
    weights,
    mat_sem,
    g_send,
    g_recv,
    w_send,
    w_recv,
    x_send,
    x_recv,
    s_send,
    s_recv,
):
    tiles, chunks, rows_n, side, sections, owned, hits = sizes
    stages = 2 * sections
    me_t = lax.axis_index("tile")
    me_s = lax.axis_index("sub")

    def partner(bit):
        width = 1 << bit
        return me_s + width - 2 * width * ((me_s // width) % 2)

    bits = [sections - 1 - n if n < sections else n - sections for n in range(stages)]

    def mat_copy(which, k, i):
        ref = own_ref if which == 0 else pair_ref
        return pltpu.make_async_copy(
            ref.at[k, :, pl.ds(i * side, side)], spread.at[me_t, which * sections + k, i], mat_sem.at[which, k, i]
        )

    for which in range(2):
        for k in range(sections):
            for i in range(rows_n):
                mat_copy(which, k, i).start()

    barrier = pltpu.get_barrier_semaphore()
    for d in range(1, tiles):
        pl.semaphore_signal(
            barrier, inc=1, device_id={"tile": (me_t + d) % tiles}, device_id_type=MESH
        )
    for bit in range(sections):
        pl.semaphore_signal(barrier, inc=1, device_id={"sub": partner(bit)}, device_id_type=MESH)

    def convert(u, carry):
        for p in range(2):
            region[me_t * owned + u, p] = image_ref[p, u].astype(bf16)
        return carry

    lax.fori_loop(0, owned, convert, 0)
    pl.semaphore_wait(barrier, tiles - 1 + sections)

    sibling = me_t + 1 - 2 * (me_t % 2)

    def region_copy(d, src, dest):
        return pltpu.make_async_remote_copy(
            src_ref=region.at[pl.ds(src * owned, owned)],
            dst_ref=region.at[pl.ds(src * owned, owned)],
            send_sem=g_send.at[d],
            recv_sem=g_recv.at[src],
            device_id={"tile": dest},
            device_id_type=MESH,
        )

    def weight_copy(d, src):
        dest = (me_t + d) % tiles
        return pltpu.make_async_remote_copy(
            src_ref=weight_ref.at[dest],
            dst_ref=weights.at[src],
            send_sem=w_send.at[d],
            recv_sem=w_recv.at[src],
            device_id={"tile": dest},
            device_id_type=MESH,
        )

    for d in range(2, tiles, 2):
        region_copy(d, me_t, (me_t + d) % tiles).start()
    region_copy(1, me_t, sibling).start()
    weights[me_t] = weight_ref[me_t]
    beam_t_ref[...] = beam_ref[...].astype(f32).T.astype(bf16)
    range_t_ref[...] = range_ref[...].astype(f32).T.astype(bf16)

    base = lax.convert_element_type(me_t * (chunks * side), f32)
    total_range = tiles * chunks * side

    def prepare(k):
        for i in range(rows_n):
            for which in range(2):
                mat_copy(which, k, i).wait()

        def build(i, carry):
            col = lax.broadcasted_iota(jnp.int32, (side, side), 1).astype(f32)
            rho = (base + col + 0.5) / total_range
            row = angle_ref[pl.ds(k * rows_n + i, 1)]
            delta = row * (side / total_range)
            theta = jnp.broadcast_to(row, (side, side)).T * rho
            turn_ref[0, k, i] = jnp.broadcast_to(jnp.cos(delta), (side, side)).T
            turn_ref[1, k, i] = jnp.broadcast_to(jnp.sin(delta), (side, side)).T
            c, s = jnp.cos(theta), jnp.sin(theta)
            phases[sections - 1 - k, 0, i] = c
            phases[sections - 1 - k, 1, i] = s
            phases[sections + k, 0, i] = c
            phases[sections + k, 1, i] = s
            for which in range(2):
                slot = which * sections + k
                real = spread[me_t, slot, i, 0]
                imag = spread[me_t, slot, i, 1]
                real_t = real.astype(f32).T.astype(bf16)
                imag_t = imag.astype(f32).T.astype(bf16)
                lo = 2 * side * which
                back_mat[k, i, pl.ds(lo, side), pl.ds(0, side)] = real_t
                back_mat[k, i, pl.ds(lo, side), pl.ds(side, side)] = imag_t
                back_mat[k, i, pl.ds(lo + side, side), pl.ds(0, side)] = -imag_t
                back_mat[k, i, pl.ds(lo + side, side), pl.ds(side, side)] = real_t
                fore_mat[k, i, pl.ds(0, side), pl.ds(lo, side)] = real
                fore_mat[k, i, pl.ds(0, side), pl.ds(lo + side, side)] = -imag
                fore_mat[k, i, pl.ds(side, side), pl.ds(lo, side)] = imag
                fore_mat[k, i, pl.ds(side, side), pl.ds(lo + side, side)] = real
            return carry

        lax.fori_loop(0, rows_n, build, 0)

    prepare(sections - 1)
    for d in range(2, tiles, 2):
        src = (me_t + d) % tiles
        region_copy(d, src, src).wait_recv()
        region_copy(d + 1, src, sibling).start()

    def zero(u, carry):
        total[u] = jnp.zeros_like(total[u])
        return carry

    lax.fori_loop(0, owned, zero, 0)

    for d in range(2, tiles, 2):
        region_copy(d + 1, (sibling + d) % tiles, sibling).wait_recv()
    region_copy(1, sibling, sibling).wait_recv()
    for d in range(1, tiles):
        weight_copy(d, me_t).start()

    share = rows_n // PARTS

    def exchange(n, c, part):
        rows = pl.ds(part * share, share)
        return pltpu.make_async_remote_copy(
            src_ref=sendbuf.at[c, rows],
            dst_ref=recvbuf.at[n, c, rows],
            send_sem=x_send.at[n, c, part],
            recv_sem=x_recv.at[n, c, part],
            device_id={"sub": partner(bits[n])},
            device_id_type=MESH,
        )

    def dot(a, b):
        return jnp.dot(a, b, preferred_element_type=f32)

    def advance(n, i, k):
        c, s = phases[n, 0, i], phases[n, 1, i]
        dc, ds = turn_ref[0, k, i], turn_ref[1, k, i]
        phases[n, 0, i] = c * dc - s * ds
        phases[n, 1, i] = s * dc + c * ds
        return c, s

    def merge_back(n, c, i, level_real, level_imag):
        k = bits[n]
        pc, ps = advance(n, i, k)
        lr, li = level_real.astype(f32), level_imag.astype(f32)
        turned = jnp.concatenate([pc * lr + ps * li, pc * li - ps * lr], axis=0).astype(bf16)
        out = dot(back_mat[k, i], turned)
        held[c, i] = out[: 2 * side].reshape(2, side, side)
        sendbuf[c, i] = out[2 * side :].astype(bf16).reshape(2, side, side)

    def stage_first(c):
        def body(i, carry):
            real = jnp.zeros((side, side), f32)
            imag = jnp.zeros((side, side), f32)
            for h in range(hits):
                q = map_ref[i, c, h]
                cc, ss = route_ref[0, i, c, h], route_ref[1, i, c, h]
                pr = region[q, 0].astype(f32)
                pi = region[q, 1].astype(f32)
                real += cc * pr + ss * pi
                imag += cc * pi - ss * pr
            routed = jnp.concatenate([real, imag], axis=0).astype(bf16)
            half = dot(routed, range_t_ref[...]).astype(bf16)
            polar_r = dot(beam_t_ref[...], half[:side]).astype(bf16)
            polar_i = dot(beam_t_ref[...], half[side:]).astype(bf16)
            merge_back(0, c, i, polar_r, polar_i)
            return carry

        for part in range(PARTS):
            lax.fori_loop(part * share, (part + 1) * share, body, 0)
            exchange(0, c, part).start()

    def stage_back(n, c):

        def body(i, carry):
            level = (held[c, i] + recvbuf[n - 1, c, i].astype(f32)).astype(bf16)
            merge_back(n, c, i, level[0], level[1])
            return carry

        for part in range(PARTS):
            exchange(n - 1, c, part).wait()
            lax.fori_loop(part * share, (part + 1) * share, body, 0)
            exchange(n, c, part).start()

    def stage_residual(c):
        n = sections
        cols = pl.ds(pl.multiple_of(c * side, side), side)

        def body(i, carry):
            rows = pl.ds(pl.multiple_of(i * side, side), side)
            level = (held[c, i] + recvbuf[n - 1, c, i].astype(f32)).astype(bf16)
            res = (level.astype(f32) - echoes_ref[:, rows, cols].astype(f32)).astype(bf16)
            residual_ref[:, rows, cols] = res
            sendbuf[c, i] = res
            return carry

        for part in range(PARTS):
            exchange(n - 1, c, part).wait()
            lax.fori_loop(part * share, (part + 1) * share, body, 0)
            exchange(n, c, part).start()

    def merge_fore(n, c, i):
        k = bits[n]
        values = jnp.concatenate(
            [
                sendbuf[c, i].reshape(2 * side, side),
                recvbuf[n, c, i].reshape(2 * side, side),
            ],
            axis=0,
        )
        mixed = dot(fore_mat[k, i], values)
        mr, mi = mixed[:side], mixed[side:]
        pc, ps = advance(n, i, k)
        return jnp.concatenate([pc * mr - ps * mi, pc * mi + ps * mr], axis=0).astype(bf16)

    def stage_fore(n, c):

        def body(i, carry):
            sendbuf[c, i] = merge_fore(n, c, i).reshape(2, side, side)
            return carry

        for part in range(PARTS):
            exchange(n, c, part).wait()
            lax.fori_loop(part * share, (part + 1) * share, body, 0)
            exchange(n + 1, c, part).start()

    def spread_copy(d, src, dest, c):
        return pltpu.make_async_remote_copy(
            src_ref=spread.at[src, c],
            dst_ref=spread.at[src, c],
            send_sem=s_send.at[d, c],
            recv_sem=s_recv.at[src, c],
            device_id={"tile": dest},
            device_id_type=MESH,
        )

    def stage_last(c):
        n = stages - 1

        def body(i, carry):
            field = merge_fore(n, c, i)
            beamed = jnp.concatenate(
                [dot(beam_ref[...], field[:side]), dot(beam_ref[...], field[side:])], axis=0
            ).astype(bf16)
            out = dot(beamed, range_ref[...]).astype(bf16)
            spread[me_t, c, i] = out.reshape(2, side, side)
            return carry

        for part in range(PARTS):
            exchange(n, c, part).wait()
            lax.fori_loop(part * share, (part + 1) * share, body, 0)
        for d in range(2, tiles, 2):
            spread_copy(d, me_t, (me_t + d) % tiles, c).start()
        spread_copy(1, me_t, sibling, c).start()

    def stage_relay(c):
        for d in range(2, tiles, 2):
            src = (me_t + d) % tiles
            spread_copy(d, src, src, c).wait_recv()
            spread_copy(d + 1, src, sibling, c).start()

    height = 16

    def stage_gather(c):
        for d in range(2, tiles, 2):
            spread_copy(d + 1, (sibling + d) % tiles, sibling, c).wait_recv()
        spread_copy(1, sibling, sibling, c).wait_recv()

        @pl.when(c == 0)
        def _():
            for d in range(1, tiles):
                weight_copy(d, (me_t + d) % tiles).wait_recv()

        def body(b, carry):
            rows = pl.ds(pl.multiple_of(b * height, height), height)
            reals = [total[u, 0, rows] for u in range(owned)]
            imags = [total[u, 1, rows] for u in range(owned)]

            def add(t, sums):
                reals, imags = list(sums[0]), list(sums[1])
                for i in range(rows_n):
                    sr = spread[t, c, i, 0, rows].astype(f32)
                    si = spread[t, c, i, 1, rows].astype(f32)
                    for u in range(owned):
                        wc = weights[t, 0, c * rows_n + i, pl.ds(u, 1)]
                        ws = weights[t, 1, c * rows_n + i, pl.ds(u, 1)]
                        reals[u] += wc * sr - ws * si
                        imags[u] += wc * si + ws * sr
                return tuple(reals), tuple(imags)

            reals, imags = lax.fori_loop(0, tiles, add, (tuple(reals), tuple(imags)))
            for u in range(owned):
                total[u, 0, rows] = reals[u]
                total[u, 1, rows] = imags[u]
            return carry

        lax.fori_loop(0, side // height, body, 0)

    runs = [stage_first]
    for n in range(1, sections):
        runs.append(functools.partial(stage_back, n))
    runs.append(stage_residual)
    for n in range(sections, stages - 1):
        runs.append(functools.partial(stage_fore, n))
    runs.append(stage_last)
    runs.append(stage_relay)
    runs.append(stage_gather)

    def step(t, carry):
        order = list(zip(runs, LAGS))
        for run, lag in [order[1], order[0]] + order[2:]:
            c = t - lag

            @pl.when((c >= 0) & (c < chunks))
            def _():
                run(c)

            if run is stage_first:

                @pl.when(t == 0)
                def _():
                    for k in reversed(range(sections - 1)):
                        prepare(k)

        return carry

    lax.fori_loop(0, chunks + LAGS[-1], step, 0)

    def finish(u, carry):
        for p in range(2):
            new_ref[p, u] = image_ref[p, u] - step_length * total[u, p]
        return carry

    lax.fori_loop(0, owned, finish, 0)

    for d in range(1, tiles):
        region_copy(d, me_t, sibling).wait_send()
        weight_copy(d, me_t).wait_send()

    def drain(c, carry):
        for d in range(1, tiles):
            spread_copy(d, me_t, sibling, c).wait_send()
        return carry

    lax.fori_loop(0, chunks, drain, 0)


def per_device(
    echoes,
    image,
    merge_own,
    merge_pair,
    merge_angle,
    beam_kernel,
    range_kernel,
    block_map,
    route_angle,
):
    side = beam_kernel.shape[0]
    sections = merge_own.shape[0]
    rows_n, chunks, hits = block_map.shape
    tiles = lax.axis_size("tile")
    owned = image.shape[1]
    stages = 2 * sections

    route_cos = jnp.cos(route_angle)
    route_sin = jnp.sin(route_angle)
    region_count = tiles * owned
    matched = (block_map[..., None] == jnp.arange(region_count)).astype(f32)
    one = jnp.stack(
        [
            jnp.sum(matched * route_cos[..., None], axis=2),
            jnp.sum(matched * route_sin[..., None], axis=2),
        ]
    )
    one = one.reshape(2, rows_n, chunks, tiles, owned).transpose(3, 0, 2, 1, 4)
    weight = jnp.broadcast_to(
        one.reshape(tiles, 2, chunks * rows_n, owned, 1),
        (tiles, 2, chunks * rows_n, owned, side),
    )
    smem = pl.BlockSpec(memory_space=pltpu.SMEM)
    vmem = pl.BlockSpec(memory_space=pltpu.VMEM)
    hbm = pl.BlockSpec(memory_space=pl.ANY)
    block = (2, side, side)
    dma = pltpu.SemaphoreType.DMA
    return pl.pallas_call(
        functools.partial(kernel, (tiles, chunks, rows_n, side, sections, owned, hits)),
        out_shape=(
            jax.ShapeDtypeStruct(image.shape, f32),
            jax.ShapeDtypeStruct(echoes.shape, bf16),
        ),
        in_specs=[smem] * 2 + [vmem, vmem, hbm, hbm] + [vmem] * 4,
        out_specs=(vmem, vmem),
        scratch_shapes=[
            pltpu.VMEM((side, side), bf16),
            pltpu.VMEM((side, side), bf16),
            pltpu.VMEM((2, sections, rows_n, side, side), f32),
            pltpu.VMEM((region_count,) + block, bf16),
            pltpu.VMEM((sections, rows_n, 4 * side, 2 * side), bf16),
            pltpu.VMEM((sections, rows_n, 2 * side, 4 * side), bf16),
            pltpu.VMEM((stages, 2, rows_n, side, side), f32),
            pltpu.VMEM((chunks, rows_n) + block, f32),
            pltpu.VMEM((chunks, rows_n) + block, bf16),
            pltpu.VMEM((stages, chunks, rows_n) + block, bf16),
            pltpu.VMEM((tiles, chunks, rows_n) + block, bf16),
            pltpu.VMEM((owned,) + block, f32),
            pltpu.VMEM((tiles, 2, chunks * rows_n, owned, side), f32),
            dma((2, sections, rows_n)),
            dma((tiles,)),
            dma((tiles,)),
            dma((tiles,)),
            dma((tiles,)),
            dma((stages, chunks, PARTS)),
            dma((stages, chunks, PARTS)),
            dma((tiles, chunks)),
            dma((tiles, chunks)),
        ],
        compiler_params=pltpu.CompilerParams(
            collective_id=0, has_side_effects=True, vmem_limit_bytes=63 * 1024 * 1024
        ),
    )(
        block_map,
        jnp.stack([route_cos, route_sin]),
        echoes,
        image,
        merge_own,
        merge_pair,
        merge_angle.reshape(sections * rows_n, side),
        beam_kernel,
        range_kernel,
        weight,
    )


def solution(mesh):
    return jax.shard_map(
        per_device,
        mesh=mesh,
        in_specs=(
            P(None, "sub", "tile"),
            P(None, ("sub", "tile"), None, None),
            P(None, None, "sub", None),
            P(None, None, "sub", None),
            P(None, "sub"),
            P(),
            P(),
            P("sub", "tile", None),
            P("sub", "tile", None),
        ),
        out_specs=(P(None, ("sub", "tile"), None, None), P(None, "sub", "tile")),
        check_vma=False,
    )
```
